32 devices in a mesh: query: 2 (over x), gallery: 16 (over z, y, core).
Axes of the slice: x: 2, y: 2, z: 4, core: 2. Of those that a mesh axis runs over, the one named last changes fastest.
Arguments:
- query_hidden: bfloat16 [768, 32, 768], P(('query', 'gallery')), may hold values from -6 to 6
- query_mask: int32 [768, 32], P(('query', 'gallery')), may hold values 0 or 1
- passage_hidden: bfloat16 [16, 360, 768], P('gallery', 'query'), may hold values from -6 to 6
- passage_ids: int32 [16, 360], P('gallery', 'query'), may hold values from 999 to 30521, as said below
- passage_lengths: int32 [32], P('gallery'), may hold values from 30 to 180, as said below
- projection: bfloat16 [768, 128], replicated, may hold values from -0.21875 to 0.21875
Outputs:
- scores: float32 [768, 32], P(('query', 'gallery'))
The draws below stay inside these ranges and needn't reach their ends.
Inputs may be any that keep to these rules, and one draw needn't show every extreme that they name: `passage_ids`: ids from 999 to 1066 are punctuation; the rest are words. `passage_lengths`: some passage has exactly 180 tokens.
All inputs are finite; a program needn't handle non-finite values. No bound on the sum of `query_mask` on one device may be relied on, other than what follows from the above.
Results may differ from the reference program's by a relative error of at most 0.00036.
Values may be sent and summed in bfloat16 or wider, within the bound.
A program may use at most 64 MiB of HBM per device.

```python
import jax
import jax.numpy as jnp
from jax import lax

D = 768
DIM = 128
VOCAB = 30522
PLEN = 180
QLEN = 32
PUNCT_LO = 999
PUNCT_HI = 1067
QRY_DEV = 24
PASS_GRP = 2
GROUPS = 16
PASSAGES = 32
QUERIES = 768


def draw_passage_ids(key, part):
    key_first, key_second, key_third = jax.random.split(jax.random.fold_in(key, 71), 3)
    id_shape = (GROUPS, PASS_GRP * PLEN)
    word_ids = jax.random.randint(key_first, id_shape, PUNCT_HI, VOCAB, dtype=jnp.int32)
    mark_ids = jax.random.randint(key_second, id_shape, PUNCT_LO, PUNCT_HI, dtype=jnp.int32)
    chosen = jax.random.randint(key_third, id_shape, 0, 100, dtype=jnp.int32) < 15
    return jnp.where(chosen, mark_ids, word_ids)


def draw_passage_lengths(key, part):
    key_first, key_second, key_third = jax.random.split(jax.random.fold_in(key, 83), 3)
    shortest = PLEN // 6
    lengths = jax.random.randint(key_first, (PASSAGES,), shortest, PLEN + 1, dtype=jnp.int32)
    longest_at = jax.random.randint(key_second, (), 0, PASSAGES, dtype=jnp.int32)
    shortest_at = (longest_at + 1 + jax.random.randint(key_third, (), 0, PASSAGES - 1, dtype=jnp.int32)) % PASSAGES
    return lengths.at[longest_at].set(PLEN).at[shortest_at].set(shortest)


def touch_ends(drawn, stream_key, smallest, high):
    longest = drawn.shape.index(max(drawn.shape))
    spots = []
    for shift in (0, 1):
        where = [jax.random.randint(jax.random.fold_in(stream_key, axis), (), 0, length) for axis, length in enumerate(drawn.shape)]
        where[longest] = (where[longest] + shift) % drawn.shape[longest]
        spots.append(tuple(where))
    return drawn.at[spots[0]].set(smallest).at[spots[1]].set(high)


def shard_levels(own_key, shape, cuts, low, largest):
    def one(dim, shards_of):
        draws = jax.random.uniform(jax.random.fold_in(jax.random.fold_in(own_key, 6), dim), (shards_of,), jnp.float32, low / len(cuts), largest / len(cuts))
        return jnp.repeat(jnp.exp(draws), shape[dim] // shards_of).reshape((-1,) + (1,) * (len(shape) - dim - 1))

    factor_of = one(*cuts[0])
    for cut in cuts[1:]:
        factor_of = factor_of * one(*cut)
    return factor_of


def bell_draw(stream_key, shape, spread, most, pieces=(), kind=jnp.bfloat16):
    factor_of = shard_levels(stream_key, shape, pieces, -0.22, 0.18) if pieces else 1.0
    result = jax.random.normal(stream_key, shape, jnp.float32) * spread * factor_of
    return jnp.minimum(jnp.maximum(result, -most), most).astype(kind)


def setup_inputs(seed: int = 0) -> dict:
    streams_of = jax.random.split(jax.random.key(seed), 7)
    query_hidden = bell_draw(streams_of[0], (QUERIES, QLEN, D), 1.0, 6.0, ((0, 32),))
    query_mask = touch_ends((jax.random.randint(streams_of[1], (QUERIES, QLEN), 0, 4) < 3).astype(jnp.int32), jax.random.fold_in(streams_of[1], 1), 0, 1)
    passage_hidden = bell_draw(streams_of[2], (GROUPS, PASS_GRP * PLEN, D), 1.0, 6.0, ((0, 16), (1, 2)))
    passage_ids = draw_passage_ids(jax.random.fold_in(streams_of[6], 71), 0)
    passage_lengths = draw_passage_lengths(jax.random.fold_in(streams_of[6], 71), 0)
    projection = bell_draw(streams_of[5], (D, DIM), D ** -0.5, 0.21875)
    return {"query_hidden": query_hidden, "query_mask": query_mask, "passage_hidden": passage_hidden, "passage_ids": passage_ids, "passage_lengths": passage_lengths, "projection": projection}


EPS = 1e-06
NEG = -1000000000.0

def unit_rows(hidden, projection):
    flat_rows = hidden.reshape(-1, hidden.shape[-1])
    projected = jnp.dot(flat_rows, projection, preferred_element_type=jnp.float32)
    inverse_norm = lax.rsqrt(lax.optimization_barrier(jnp.sum(projected * projected, axis=-1, keepdims=True)) + EPS)
    return (projected * inverse_norm).astype(jnp.bfloat16)

def reference(query_hidden, query_mask, passage_hidden, passage_ids, passage_lengths, projection):
    passage_unit = unit_rows(passage_hidden, projection)
    token_pos = jnp.arange(PLEN, dtype=jnp.int32)[None, :]
    token_ids = passage_ids.reshape(PASSAGES, PLEN)
    punctuation = (token_ids >= PUNCT_LO) & (token_ids < PUNCT_HI)
    kept = (token_pos < passage_lengths[:, None]) & ((token_pos == 0) | jnp.logical_not(punctuation))
    kept_flat = kept.reshape(1, PASSAGES * PLEN)
    query_unit = unit_rows(query_hidden, projection).reshape(-1, QRY_DEV * QLEN, DIM)
    weights = query_mask.astype(jnp.float32).reshape(-1, QRY_DEV, QLEN)

    def score_block(block_pair):
        query_rows, mask_rows = block_pair
        similar = jnp.dot(query_rows, passage_unit.T, preferred_element_type=jnp.float32)
        similar = jnp.where(kept_flat, similar, NEG).reshape(-1, PASSAGES, PLEN)
        running = lax.optimization_barrier(jnp.max(similar, axis=2)).reshape(QRY_DEV, QLEN, PASSAGES)
        return lax.optimization_barrier(jnp.sum(running * mask_rows[:, :, None], axis=1))
    return lax.map(score_block, (query_unit, weights)).reshape(QUERIES, PASSAGES)
```

```python
import math

import jax
import jax.numpy as jnp
from jax import lax
from jax.experimental import pallas as pl
from jax.experimental.pallas import tpu as pltpu
from jax.sharding import PartitionSpec as P

DIM = 128
PLEN = 180
QLEN = 32
PUNCT_LO = 999
PUNCT_HI = 1067
PASS_GRP = 2


EPS = 1e-06
NEG = -1000000000.0


def unit_rows(hidden, projection):
    flat_rows = hidden.reshape(-1, hidden.shape[-1])
    projected = jnp.dot(flat_rows, projection, preferred_element_type=jnp.float32)
    inverse_norm = lax.rsqrt(jnp.sum(projected * projected, axis=-1, keepdims=True) + EPS)
    return (projected * inverse_norm).astype(jnp.bfloat16)


def local(query_hidden, query_mask, passage_hidden, passage_ids, passage_lengths, projection):
    row_count = passage_hidden.shape[1]
    query_count = query_hidden.shape[0]
    groups = lax.axis_size("gallery")
    query_block = lax.axis_index("query")
    position = query_block * row_count + jnp.arange(row_count, dtype=jnp.int32)
    passage_slot = position // PLEN
    token_pos = position % PLEN
    onehot = passage_slot[:, None] == jnp.arange(PASS_GRP, dtype=jnp.int32)[None, :]
    length_rows = jnp.sum(jnp.where(onehot, passage_lengths[None, :], 0), axis=1)
    token_ids = passage_ids[0]
    punctuation = (token_ids >= PUNCT_LO) & (token_ids < PUNCT_HI)
    kept = (token_pos < length_rows) & ((token_pos == 0) | jnp.logical_not(punctuation))
    kept_flag = kept.astype(jnp.bfloat16)[None, :]
    passage_unit = unit_rows(passage_hidden, projection).reshape(1, row_count, DIM)
    query_unit = unit_rows(query_hidden, projection)
    weights = query_mask.astype(jnp.float32).reshape(-1)
    thin_units, thin_flags = (
        lax.all_gather(passage_unit, "gallery", axis=0, tiled=True),
        lax.all_gather(kept_flag, "gallery", axis=0, tiled=True),
    )
    initial = jnp.full((query_unit.shape[0], groups * PASS_GRP), NEG, jnp.float32)
    piece_units = lax.all_gather(thin_units, "query", axis=1, tiled=True)
    piece_flags = lax.all_gather(thin_flags, "query", axis=1, tiled=True)
    piece_rows = piece_units.shape[1]
    row_slot = jnp.arange(piece_rows, dtype=jnp.int32) // PLEN
    block_width = math.gcd(groups, 4)
    unit_blocks = piece_units.reshape(groups // block_width, block_width * piece_rows, DIM)
    flag_blocks = piece_flags.reshape(groups // block_width, 1, block_width * piece_rows)

    def one_block(block_pair):
        unit_block, flag_block = block_pair
        similar = jnp.einsum(
            "td,rd->tr", query_unit, unit_block, preferred_element_type=jnp.float32
        )
        similar = jnp.where(flag_block > 0, similar, NEG).reshape(-1, block_width, piece_rows)
        per_member = [
            jnp.max(jnp.where(row_slot == member, similar, NEG), axis=2)
            for member in range(PASS_GRP)
        ]
        return jnp.stack(per_member, axis=2)

    fresh_max = lax.map(one_block, (unit_blocks, flag_blocks))
    fresh_max = jnp.transpose(fresh_max, (1, 0, 2, 3)).reshape(initial.shape)
    running = jnp.maximum(initial, fresh_max)
    scores = jnp.sum(
        (running * weights[:, None]).reshape(query_count, QLEN, groups * PASS_GRP), axis=1
    )
    return scores


ROWS = 192
HALF = 96
MESH = pl.DeviceIdType.MESH


def fused_kernel(
    qh_hbm, mask_hbm, ph_hbm, ids_hbm, len_hbm, proj_hbm, out_ref,
    qh, mask, ph, ids, lens, proj, padded, blocks, queries, best, part_out, part_in,
    in_sem, z_send, z_recv, n_send, n_recv, c_send, c_recv,
):
    x = lax.axis_index("query")
    g = lax.axis_index("gallery")
    core = g % 2
    y = (g // 2) % 2
    z = g // 4
    rows = ph.shape[0]
    qcount, qlen = mask.shape
    width = qcount * qlen

    def at(zz, yy, cc):
        return (zz * 2 + yy) * 2 + cc

    line = [(x, at((z + 4 - d) % 4, y, core)) for d in range(4)]
    x_near = (1 - x, g)
    y_near = (x, at(z, 1 - y, core))
    twin = (x, at(z, y, 1 - core))

    barrier = pltpu.get_barrier_semaphore()
    for peer in (line[1], line[2], line[3], x_near, y_near, twin):
        pl.semaphore_signal(barrier, inc=1, device_id=peer, device_id_type=MESH)

    loads = [
        pltpu.make_async_copy(src, dst, in_sem.at[k])
        for k, (src, dst) in enumerate(
            [(ph_hbm.at[0], ph), (proj_hbm, proj), (ids_hbm, ids), (len_hbm, lens), (mask_hbm, mask), (qh_hbm, qh)]
        )
    ]
    for load in loads:
        load.start()
    best[...] = jnp.zeros(best.shape, jnp.float32)

    for load in loads[:4]:
        load.wait()
    projected = jnp.dot(ph[...], proj[...], preferred_element_type=jnp.float32)
    unit = projected * lax.rsqrt(jnp.sum(projected * projected, axis=-1, keepdims=True) + EPS)
    tokens = ids[...]
    slot = lax.broadcasted_iota(jnp.int32, tokens.shape, 1)
    punctuation = (tokens >= PUNCT_LO) & (tokens < PUNCT_HI)
    kept = (slot < lens[x]) & ((slot == 0) | jnp.logical_not(punctuation))
    kept = jnp.where(kept, 1.0, 0.0)
    eye = lax.broadcasted_iota(jnp.int32, (rows, rows), 0) == lax.broadcasted_iota(jnp.int32, (rows, rows), 1)
    column = jnp.sum(jnp.where(eye, jnp.broadcast_to(kept, (rows, rows)), 0.0), axis=1, keepdims=True)
    first = unit[0:1, :]
    padded[...] = jnp.broadcast_to(first, padded.shape)
    padded[pl.ds(0, rows), :] = jnp.where(column > 0.0, unit, first)
    blocks[0] = padded[...].astype(jnp.bfloat16)

    pl.semaphore_wait(barrier, 6)

    def remote(src, dst, send, recv, peer):
        return pltpu.make_async_remote_copy(
            src_ref=src, dst_ref=dst, send_sem=send, recv_sem=recv, device_id=peer, device_id_type=MESH
        )

    along_z = {
        d: remote(blocks.at[0], blocks.at[4 * d], z_send.at[d], z_recv.at[d], line[d]) for d in (1, 2, 3)
    }

    def near(d, kind):
        if kind == 0:
            pair, peer = (blocks.at[4 * d], blocks.at[4 * d + 2]), x_near
        elif kind == 1:
            pair, peer = (blocks.at[4 * d], blocks.at[4 * d + 1]), y_near
        elif kind == 2:
            half = pl.ds(0, HALF)
            pair, peer = (blocks.at[4 * d + 2, half], blocks.at[4 * d + 3, half]), y_near
        else:
            half = pl.ds(HALF, HALF)
            pair, peer = (blocks.at[4 * d + 1, half], blocks.at[4 * d + 3, half]), x_near
        k = 4 * d + kind
        return remote(*pair, n_send.at[k], n_recv.at[k], peer)

    side = {(d, kind): near(d, kind) for d in range(4) for kind in range(4)}

    def score(d, dx, dy):
        passage = ((((z + d) % 4) * 2 + (y + dy) % 2) * 2 + core) * 2 + (x + dx) % 2
        held = 4 * d + 2 * dx + dy

        def chunk(k, carry):
            cols = pl.ds(pl.multiple_of(k * 256, 256), 256)
            similar = jnp.dot(blocks[held], queries[:, cols], preferred_element_type=jnp.float32)
            best[pl.ds(passage, 1), cols] = jnp.max(similar, axis=0, keepdims=True)
            return carry

        lax.fori_loop(0, 2 * width // 256, chunk, 0)

    side[0, 0].start()
    side[0, 1].start()
    along_z[1].start()
    along_z[3].start()
    along_z[2].start()

    loads[4].wait()
    flags = mask[...].astype(jnp.float32)
    spread = lax.broadcasted_iota(jnp.int32, (qlen, width), 1) % qlen == lax.broadcasted_iota(jnp.int32, (qlen, width), 0)
    spread = jnp.dot(flags, jnp.where(spread, 1.0, 0.0), preferred_element_type=jnp.float32)
    member = lax.broadcasted_iota(jnp.int32, (qcount, width), 1) // qlen == lax.broadcasted_iota(jnp.int32, (qcount, width), 0)
    weight = jnp.sum(jnp.where(member, spread, 0.0), axis=0, keepdims=True)
    loads[5].wait()
    for k in range(width // 256):
        cols = slice(k * 256, (k + 1) * 256)
        projected = jnp.dot(qh[cols, :], proj[...], preferred_element_type=jnp.float32).T
        unit = projected * lax.rsqrt(jnp.sum(projected * projected, axis=0, keepdims=True) + EPS)
        queries[:, cols] = (unit * weight[:, cols]).astype(jnp.bfloat16)
    own, other = pl.ds(0, width), pl.ds(width, width)
    swap = remote(queries.at[:, own], queries.at[:, other], c_send.at[0], c_recv.at[0], twin)
    swap.start()

    def pass_on(d):
        side[d, 0].wait_recv()
        side[d, 2].start()
        side[d, 1].wait_recv()
        side[d, 3].start()

    def corner(d):
        side[d, 2].wait_recv()
        side[d, 3].wait_recv()
        score(d, 1, 1)

    def from_line(d):
        along_z[d].wait_recv()
        side[d, 0].start()
        side[d, 1].start()

    pass_on(0)
    from_line(1)
    from_line(3)
    swap.wait_recv()
    score(0, 0, 0)
    score(0, 1, 0)
    score(0, 0, 1)
    from_line(2)
    score(1, 0, 0)
    score(3, 0, 0)
    corner(0)
    pass_on(1)
    score(1, 1, 0)
    score(1, 0, 1)
    pass_on(3)
    score(3, 1, 0)
    score(3, 0, 1)
    score(2, 0, 0)
    pass_on(2)
    score(2, 1, 0)
    score(2, 0, 1)
    corner(1)
    corner(3)
    corner(2)

    group = jnp.where(member, 1.0, 0.0).astype(jnp.bfloat16)

    def total(values):
        high = values.astype(jnp.bfloat16)
        low = (values - high.astype(jnp.float32)).astype(jnp.bfloat16)
        dims = (((1,), (1,)), ((), ()))
        return lax.dot_general(group, high, dims, preferred_element_type=jnp.float32) + lax.dot_general(
            group, low, dims, preferred_element_type=jnp.float32
        )

    part_out[...] = total(best[:, width : 2 * width])
    back = remote(part_out, part_in, c_send.at[1], c_recv.at[1], twin)
    back.start()
    mine = total(best[:, 0:width])
    for copy in list(along_z.values()) + list(side.values()) + [swap]:
        copy.wait_send()
    back.wait()
    out_ref[...] = mine + part_in[...]


def fused(query_hidden, query_mask, passage_hidden, passage_ids, passage_lengths, projection):
    qcount, qlen, depth = query_hidden.shape
    width = qcount * qlen
    rows = passage_hidden.shape[1]
    passages = PASS_GRP * lax.axis_size("gallery")
    anywhere = pl.BlockSpec(memory_space=pltpu.HBM)
    dma = pltpu.SemaphoreType.DMA
    bf16, f32 = jnp.bfloat16, jnp.float32
    return pl.pallas_call(
        fused_kernel,
        out_shape=jax.ShapeDtypeStruct((qcount, passages), f32),
        in_specs=[anywhere] * 6,
        out_specs=pl.BlockSpec(memory_space=pltpu.VMEM),
        scratch_shapes=[
            pltpu.VMEM((width, depth), bf16),
            pltpu.VMEM((qcount, qlen), jnp.int32),
            pltpu.VMEM((rows, depth), bf16),
            pltpu.VMEM((1, rows), jnp.int32),
            pltpu.SMEM(passage_lengths.shape, jnp.int32),
            pltpu.VMEM((depth, DIM), bf16),
            pltpu.VMEM((ROWS, DIM), f32),
            pltpu.VMEM((16, ROWS, DIM), bf16),
            pltpu.VMEM((DIM, 2 * width), bf16),
            pltpu.VMEM((passages, 2 * width), f32),
            pltpu.VMEM((qcount, passages), f32),
            pltpu.VMEM((qcount, passages), f32),
            dma((6,)), dma((4,)), dma((4,)), dma((16,)), dma((16,)), dma((2,)), dma((2,)),
        ],
        compiler_params=pltpu.CompilerParams(
            collective_id=0, has_side_effects=True, vmem_limit_bytes=60 * 1024 * 1024
        ),
    )(query_hidden.reshape(width, depth), query_mask, passage_hidden, passage_ids, passage_lengths, projection)


def solution(mesh):
    placed = (
        P(("query", "gallery"), None, None),
        P(("query", "gallery"), None),
        P("gallery", "query", None),
        P("gallery", "query"),
        P("gallery"),
        P(),
    )
    small = mesh.shape["query"] == PASS_GRP and mesh.shape["gallery"] == 16
    return jax.shard_map(
        fused if small else local, mesh=mesh, in_specs=placed, out_specs=P(("query", "gallery"), None), check_vma=False
    )
```

```python
import math

import jax
import jax.numpy as jnp
from jax import lax
from jax.experimental import pallas as pl
from jax.experimental.pallas import tpu as pltpu
from jax.sharding import PartitionSpec as P

DIM = 128
PLEN = 180
QLEN = 32
PUNCT_LO = 999
PUNCT_HI = 1067
PASS_GRP = 2


EPS = 1e-06
NEG = -1000000000.0


def unit_rows(hidden, projection):
    flat_rows = hidden.reshape(-1, hidden.shape[-1])
    projected = jnp.dot(flat_rows, projection, preferred_element_type=jnp.float32)
    inverse_norm = lax.rsqrt(jnp.sum(projected * projected, axis=-1, keepdims=True) + EPS)
    return (projected * inverse_norm).astype(jnp.bfloat16)


def local(query_hidden, query_mask, passage_hidden, passage_ids, passage_lengths, projection):
    row_count = passage_hidden.shape[1]
    query_count = query_hidden.shape[0]
    groups = lax.axis_size("gallery")
    query_block = lax.axis_index("query")
    position = query_block * row_count + jnp.arange(row_count, dtype=jnp.int32)
    passage_slot = position // PLEN
    token_pos = position % PLEN
    onehot = passage_slot[:, None] == jnp.arange(PASS_GRP, dtype=jnp.int32)[None, :]
    length_rows = jnp.sum(jnp.where(onehot, passage_lengths[None, :], 0), axis=1)
    token_ids = passage_ids[0]
    punctuation = (token_ids >= PUNCT_LO) & (token_ids < PUNCT_HI)
    kept = (token_pos < length_rows) & ((token_pos == 0) | jnp.logical_not(punctuation))
    kept_flag = kept.astype(jnp.bfloat16)[None, :]
    passage_unit = unit_rows(passage_hidden, projection).reshape(1, row_count, DIM)
    query_unit = unit_rows(query_hidden, projection)
    weights = query_mask.astype(jnp.float32).reshape(-1)
    thin_units, thin_flags = (
        lax.all_gather(passage_unit, "gallery", axis=0, tiled=True),
        lax.all_gather(kept_flag, "gallery", axis=0, tiled=True),
    )
    initial = jnp.full((query_unit.shape[0], groups * PASS_GRP), NEG, jnp.float32)
    piece_units = lax.all_gather(thin_units, "query", axis=1, tiled=True)
    piece_flags = lax.all_gather(thin_flags, "query", axis=1, tiled=True)
    piece_rows = piece_units.shape[1]
    row_slot = jnp.arange(piece_rows, dtype=jnp.int32) // PLEN
    block_width = math.gcd(groups, 4)
    unit_blocks = piece_units.reshape(groups // block_width, block_width * piece_rows, DIM)
    flag_blocks = piece_flags.reshape(groups // block_width, 1, block_width * piece_rows)

    def one_block(block_pair):
        unit_block, flag_block = block_pair
        similar = jnp.einsum(
            "td,rd->tr", query_unit, unit_block, preferred_element_type=jnp.float32
        )
        similar = jnp.where(flag_block > 0, similar, NEG).reshape(-1, block_width, piece_rows)
        per_member = [
            jnp.max(jnp.where(row_slot == member, similar, NEG), axis=2)
            for member in range(PASS_GRP)
        ]
        return jnp.stack(per_member, axis=2)

    fresh_max = lax.map(one_block, (unit_blocks, flag_blocks))
    fresh_max = jnp.transpose(fresh_max, (1, 0, 2, 3)).reshape(initial.shape)
    running = jnp.maximum(initial, fresh_max)
    scores = jnp.sum(
        (running * weights[:, None]).reshape(query_count, QLEN, groups * PASS_GRP), axis=1
    )
    return scores


ROWS = 192
HALF = 96
MESH = pl.DeviceIdType.MESH


def fused_kernel(
    qh_hbm, mask_hbm, ph_hbm, ids_hbm, len_hbm, proj_hbm, out_ref,
    qh, mask, ph, ids, lens, proj, padded, blocks, queries, best, part_out, part_in,
    in_sem, z_send, z_recv, n_send, n_recv, c_send, c_recv,
):
    x = lax.axis_index("query")
    g = lax.axis_index("gallery")
    core = g % 2
    y = (g // 2) % 2
    z = g // 4
    rows = ph.shape[0]
    qcount, qlen = mask.shape
    width = qcount * qlen

    def at(zz, yy, cc):
        return (zz * 2 + yy) * 2 + cc

    line = [(x, at((z + 4 - d) % 4, y, core)) for d in range(4)]
    x_near = (1 - x, g)
    y_near = (x, at(z, 1 - y, core))
    twin = (x, at(z, y, 1 - core))

    barrier = pltpu.get_barrier_semaphore()
    for peer in (line[1], line[2], line[3], x_near, y_near, twin):
        pl.semaphore_signal(barrier, inc=1, device_id=peer, device_id_type=MESH)

    loads = [
        pltpu.make_async_copy(src, dst, in_sem.at[k])
        for k, (src, dst) in enumerate(
            [(ph_hbm.at[0], ph), (proj_hbm, proj), (ids_hbm, ids), (len_hbm, lens), (mask_hbm, mask), (qh_hbm, qh)]
        )
    ]
    for load in loads:
        load.start()
    best[...] = jnp.zeros(best.shape, jnp.float32)

    for load in loads[:4]:
        load.wait()
    projected = jnp.dot(ph[...], proj[...], preferred_element_type=jnp.float32)
    unit = projected * lax.rsqrt(jnp.sum(projected * projected, axis=-1, keepdims=True) + EPS)
    tokens = ids[...]
    slot = lax.broadcasted_iota(jnp.int32, tokens.shape, 1)
    punctuation = (tokens >= PUNCT_LO) & (tokens < PUNCT_HI)
    kept = (slot < lens[x]) & ((slot == 0) | jnp.logical_not(punctuation))
    kept = jnp.where(kept, 1.0, 0.0)
    eye = lax.broadcasted_iota(jnp.int32, (rows, rows), 0) == lax.broadcasted_iota(jnp.int32, (rows, rows), 1)
    column = jnp.sum(jnp.where(eye, jnp.broadcast_to(kept, (rows, rows)), 0.0), axis=1, keepdims=True)
    first = unit[0:1, :]
    padded[...] = jnp.broadcast_to(first, padded.shape)
    padded[pl.ds(0, rows), :] = jnp.where(column > 0.0, unit, first)
    blocks[0] = padded[...].astype(jnp.bfloat16)

    pl.semaphore_wait(barrier, 6)

    def remote(src, dst, send, recv, peer):
        return pltpu.make_async_remote_copy(
            src_ref=src, dst_ref=dst, send_sem=send, recv_sem=recv, device_id=peer, device_id_type=MESH
        )

    along_z = {
        d: remote(blocks.at[0], blocks.at[4 * d], z_send.at[d], z_recv.at[d], line[d]) for d in (1, 2, 3)
    }

    def near(d, kind):
        if kind == 0:
            pair, peer = (blocks.at[4 * d], blocks.at[4 * d + 2]), x_near
        elif kind == 1:
            pair, peer = (blocks.at[4 * d], blocks.at[4 * d + 1]), y_near
        elif kind == 2:
            half = pl.ds(0, HALF)
            pair, peer = (blocks.at[4 * d + 2, half], blocks.at[4 * d + 3, half]), y_near
        else:
            half = pl.ds(HALF, HALF)
            pair, peer = (blocks.at[4 * d + 1, half], blocks.at[4 * d + 3, half]), x_near
        k = 4 * d + kind
        return remote(*pair, n_send.at[k], n_recv.at[k], peer)

    side = {(d, kind): near(d, kind) for d in range(4) for kind in range(4)}

    def score(d, dx, dy):
        passage = ((((z + d) % 4) * 2 + (y + dy) % 2) * 2 + core) * 2 + (x + dx) % 2
        held = 4 * d + 2 * dx + dy

        for k in range(2 * width // 256):
            cols = slice(k * 256, (k + 1) * 256)
            similar = jnp.dot(blocks[held], queries[:, cols], preferred_element_type=jnp.float32)
            best[pl.ds(passage, 1), cols] = jnp.max(similar, axis=0, keepdims=True)

    side[0, 0].start()
    side[0, 1].start()
    along_z[1].start()
    along_z[3].start()
    along_z[2].start()

    loads[4].wait()
    flags = mask[...].astype(jnp.float32)
    spread = lax.broadcasted_iota(jnp.int32, (qlen, width), 1) % qlen == lax.broadcasted_iota(jnp.int32, (qlen, width), 0)
    spread = jnp.dot(flags, jnp.where(spread, 1.0, 0.0), preferred_element_type=jnp.float32)
    member = lax.broadcasted_iota(jnp.int32, (qcount, width), 1) // qlen == lax.broadcasted_iota(jnp.int32, (qcount, width), 0)
    weight = jnp.sum(jnp.where(member, spread, 0.0), axis=0, keepdims=True)
    loads[5].wait()
    for k in range(width // 256):
        cols = slice(k * 256, (k + 1) * 256)
        projected = jnp.dot(qh[cols, :], proj[...], preferred_element_type=jnp.float32).T
        unit = projected * lax.rsqrt(jnp.sum(projected * projected, axis=0, keepdims=True) + EPS)
        queries[:, cols] = (unit * weight[:, cols]).astype(jnp.bfloat16)
    own, other = pl.ds(0, width), pl.ds(width, width)
    swap = remote(queries.at[:, own], queries.at[:, other], c_send.at[0], c_recv.at[0], twin)
    swap.start()

    def pass_on(d):
        side[d, 0].wait_recv()
        side[d, 2].start()
        side[d, 1].wait_recv()
        side[d, 3].start()

    def corner(d):
        side[d, 2].wait_recv()
        side[d, 3].wait_recv()
        score(d, 1, 1)

    def from_line(d):
        along_z[d].wait_recv()
        side[d, 0].start()
        side[d, 1].start()

    pass_on(0)
    from_line(1)
    from_line(3)
    swap.wait_recv()
    score(0, 0, 0)
    score(0, 1, 0)
    score(0, 0, 1)
    from_line(2)
    score(1, 0, 0)
    score(3, 0, 0)
    corner(0)
    pass_on(1)
    score(1, 1, 0)
    score(1, 0, 1)
    pass_on(3)
    score(3, 1, 0)
    score(3, 0, 1)
    score(2, 0, 0)
    pass_on(2)
    score(2, 1, 0)
    score(2, 0, 1)
    corner(1)
    corner(3)
    corner(2)

    group = jnp.where(member, 1.0, 0.0).astype(jnp.bfloat16)

    def total(values):
        high = values.astype(jnp.bfloat16)
        low = (values - high.astype(jnp.float32)).astype(jnp.bfloat16)
        dims = (((1,), (1,)), ((), ()))
        return lax.dot_general(group, high, dims, preferred_element_type=jnp.float32) + lax.dot_general(
            group, low, dims, preferred_element_type=jnp.float32
        )

    part_out[...] = total(best[:, width : 2 * width])
    back = remote(part_out, part_in, c_send.at[1], c_recv.at[1], twin)
    back.start()
    mine = total(best[:, 0:width])
    for copy in list(along_z.values()) + list(side.values()) + [swap]:
        copy.wait_send()
    back.wait()
    out_ref[...] = mine + part_in[...]


def fused(query_hidden, query_mask, passage_hidden, passage_ids, passage_lengths, projection):
    qcount, qlen, depth = query_hidden.shape
    width = qcount * qlen
    rows = passage_hidden.shape[1]
    passages = PASS_GRP * lax.axis_size("gallery")
    anywhere = pl.BlockSpec(memory_space=pltpu.HBM)
    dma = pltpu.SemaphoreType.DMA
    bf16, f32 = jnp.bfloat16, jnp.float32
    return pl.pallas_call(
        fused_kernel,
        out_shape=jax.ShapeDtypeStruct((qcount, passages), f32),
        in_specs=[anywhere] * 6,
        out_specs=pl.BlockSpec(memory_space=pltpu.VMEM),
        scratch_shapes=[
            pltpu.VMEM((width, depth), bf16),
            pltpu.VMEM((qcount, qlen), jnp.int32),
            pltpu.VMEM((rows, depth), bf16),
            pltpu.VMEM((1, rows), jnp.int32),
            pltpu.SMEM(passage_lengths.shape, jnp.int32),
            pltpu.VMEM((depth, DIM), bf16),
            pltpu.VMEM((ROWS, DIM), f32),
            pltpu.VMEM((16, ROWS, DIM), bf16),
            pltpu.VMEM((DIM, 2 * width), bf16),
            pltpu.VMEM((passages, 2 * width), f32),
            pltpu.VMEM((qcount, passages), f32),
            pltpu.VMEM((qcount, passages), f32),
            dma((6,)), dma((4,)), dma((4,)), dma((16,)), dma((16,)), dma((2,)), dma((2,)),
        ],
        compiler_params=pltpu.CompilerParams(
            collective_id=0, has_side_effects=True, vmem_limit_bytes=60 * 1024 * 1024
        ),
    )(query_hidden.reshape(width, depth), query_mask, passage_hidden, passage_ids, passage_lengths, projection)


def solution(mesh):
    placed = (
        P(("query", "gallery"), None, None),
        P(("query", "gallery"), None),
        P("gallery", "query", None),
        P("gallery", "query"),
        P("gallery"),
        P(),
    )
    small = mesh.shape["query"] == PASS_GRP and mesh.shape["gallery"] == 16
    return jax.shard_map(
        fused if small else local, mesh=mesh, in_specs=placed, out_specs=P(("query", "gallery"), None), check_vma=False
    )
```

```python
import math

import jax
import jax.numpy as jnp
from jax import lax
from jax.experimental import pallas as pl
from jax.experimental.pallas import tpu as pltpu
from jax.sharding import PartitionSpec as P

DIM = 128
PLEN = 180
QLEN = 32
PUNCT_LO = 999
PUNCT_HI = 1067
PASS_GRP = 2


EPS = 1e-06
NEG = -1000000000.0


def unit_rows(hidden, projection):
    flat_rows = hidden.reshape(-1, hidden.shape[-1])
    projected = jnp.dot(flat_rows, projection, preferred_element_type=jnp.float32)
    inverse_norm = lax.rsqrt(jnp.sum(projected * projected, axis=-1, keepdims=True) + EPS)
    return (projected * inverse_norm).astype(jnp.bfloat16)


def local(query_hidden, query_mask, passage_hidden, passage_ids, passage_lengths, projection):
    row_count = passage_hidden.shape[1]
    query_count = query_hidden.shape[0]
    groups = lax.axis_size("gallery")
    query_block = lax.axis_index("query")
    position = query_block * row_count + jnp.arange(row_count, dtype=jnp.int32)
    passage_slot = position // PLEN
    token_pos = position % PLEN
    onehot = passage_slot[:, None] == jnp.arange(PASS_GRP, dtype=jnp.int32)[None, :]
    length_rows = jnp.sum(jnp.where(onehot, passage_lengths[None, :], 0), axis=1)
    token_ids = passage_ids[0]
    punctuation = (token_ids >= PUNCT_LO) & (token_ids < PUNCT_HI)
    kept = (token_pos < length_rows) & ((token_pos == 0) | jnp.logical_not(punctuation))
    kept_flag = kept.astype(jnp.bfloat16)[None, :]
    passage_unit = unit_rows(passage_hidden, projection).reshape(1, row_count, DIM)
    query_unit = unit_rows(query_hidden, projection)
    weights = query_mask.astype(jnp.float32).reshape(-1)
    thin_units, thin_flags = (
        lax.all_gather(passage_unit, "gallery", axis=0, tiled=True),
        lax.all_gather(kept_flag, "gallery", axis=0, tiled=True),
    )
    initial = jnp.full((query_unit.shape[0], groups * PASS_GRP), NEG, jnp.float32)
    piece_units = lax.all_gather(thin_units, "query", axis=1, tiled=True)
    piece_flags = lax.all_gather(thin_flags, "query", axis=1, tiled=True)
    piece_rows = piece_units.shape[1]
    row_slot = jnp.arange(piece_rows, dtype=jnp.int32) // PLEN
    block_width = math.gcd(groups, 4)
    unit_blocks = piece_units.reshape(groups // block_width, block_width * piece_rows, DIM)
    flag_blocks = piece_flags.reshape(groups // block_width, 1, block_width * piece_rows)

    def one_block(block_pair):
        unit_block, flag_block = block_pair
        similar = jnp.einsum(
            "td,rd->tr", query_unit, unit_block, preferred_element_type=jnp.float32
        )
        similar = jnp.where(flag_block > 0, similar, NEG).reshape(-1, block_width, piece_rows)
        per_member = [
            jnp.max(jnp.where(row_slot == member, similar, NEG), axis=2)
            for member in range(PASS_GRP)
        ]
        return jnp.stack(per_member, axis=2)

    fresh_max = lax.map(one_block, (unit_blocks, flag_blocks))
    fresh_max = jnp.transpose(fresh_max, (1, 0, 2, 3)).reshape(initial.shape)
    running = jnp.maximum(initial, fresh_max)
    scores = jnp.sum(
        (running * weights[:, None]).reshape(query_count, QLEN, groups * PASS_GRP), axis=1
    )
    return scores


ROWS = 192
MESH = pl.DeviceIdType.MESH


def fused_kernel(
    qh_hbm, mask_hbm, ph_hbm, ids_hbm, len_hbm, proj_hbm, out_ref,
    qh, mask, ph, ids, lens, proj, padded, blocks, queries, best, part_out, part_in,
    in_sem, z_send, z_recv, n_send, n_recv, q_send, q_recv, p_send, p_recv,
):
    x = lax.axis_index("query")
    g = lax.axis_index("gallery")
    core = g % 2
    y = (g // 2) % 2
    z = g // 4
    rows = ph.shape[0]
    qcount, qlen = mask.shape
    width = qcount * qlen

    def at(zz, yy, cc):
        return (zz * 2 + yy) * 2 + cc

    line = [(x, at((z + 4 - d) % 4, y, core)) for d in range(4)]
    x_near = (1 - x, g)
    y_near = (x, at(z, 1 - y, core))
    twin = (x, at(z, y, 1 - core))
    x_twin = (1 - x, at(z, y, 1 - core))

    barrier = pltpu.get_barrier_semaphore()
    for peer in (line[1], line[2], line[3], x_near, y_near, twin, x_twin):
        pl.semaphore_signal(barrier, inc=1, device_id=peer, device_id_type=MESH)

    loads = [
        pltpu.make_async_copy(src, dst, in_sem.at[k])
        for k, (src, dst) in enumerate(
            [(ph_hbm.at[0], ph), (proj_hbm, proj), (ids_hbm, ids), (len_hbm, lens), (mask_hbm, mask), (qh_hbm, qh)]
        )
    ]
    for load in loads:
        load.start()
    best[...] = jnp.zeros(best.shape, jnp.float32)

    for load in loads[:4]:
        load.wait()
    projected = jnp.dot(ph[...], proj[...], preferred_element_type=jnp.float32)
    unit = projected * lax.rsqrt(jnp.sum(projected * projected, axis=-1, keepdims=True) + EPS)
    tokens = ids[...]
    slot = lax.broadcasted_iota(jnp.int32, tokens.shape, 1)
    punctuation = (tokens >= PUNCT_LO) & (tokens < PUNCT_HI)
    kept = (slot < lens[x]) & ((slot == 0) | jnp.logical_not(punctuation))
    kept = jnp.where(kept, 1.0, 0.0)
    eye = lax.broadcasted_iota(jnp.int32, (rows, rows), 0) == lax.broadcasted_iota(jnp.int32, (rows, rows), 1)
    column = jnp.sum(jnp.where(eye, jnp.broadcast_to(kept, (rows, rows)), 0.0), axis=1, keepdims=True)
    first = unit[0:1, :]
    padded[...] = jnp.broadcast_to(first, padded.shape)
    padded[pl.ds(0, rows), :] = jnp.where(column > 0.0, unit, first)
    blocks[0] = padded[...].astype(jnp.bfloat16)

    loads[4].wait()
    flags = mask[...].astype(jnp.float32)
    spread = lax.broadcasted_iota(jnp.int32, (qlen, width), 1) % qlen == lax.broadcasted_iota(jnp.int32, (qlen, width), 0)
    spread = jnp.dot(flags, jnp.where(spread, 1.0, 0.0), preferred_element_type=jnp.float32)
    member = lax.broadcasted_iota(jnp.int32, (qcount, width), 1) // qlen == lax.broadcasted_iota(jnp.int32, (qcount, width), 0)
    weight = jnp.sum(jnp.where(member, spread, 0.0), axis=0, keepdims=True)
    loads[5].wait()
    for k in range(width // 256):
        cols = slice(k * 256, (k + 1) * 256)
        projected = jnp.dot(qh[cols, :], proj[...], preferred_element_type=jnp.float32).T
        unit = projected * lax.rsqrt(jnp.sum(projected * projected, axis=0, keepdims=True) + EPS)
        queries[:, cols] = (unit * weight[:, cols]).astype(jnp.bfloat16)
    pl.semaphore_wait(barrier, 7)

    def remote(src, dst, send, recv, peer):
        return pltpu.make_async_remote_copy(
            src_ref=src, dst_ref=dst, send_sem=send, recv_sem=recv, device_id=peer, device_id_type=MESH
        )

    along_z = {
        d: remote(blocks.at[0], blocks.at[2 * d], z_send.at[d], z_recv.at[d], line[d]) for d in (1, 2, 3)
    }
    along_y = {
        d: remote(blocks.at[2 * d], blocks.at[2 * d + 1], n_send.at[d], n_recv.at[d], y_near) for d in range(4)
    }
    quarter = [pl.ds(k * width, width) for k in range(4)]

    def move(k, source, target, peer):
        return remote(queries.at[:, quarter[source]], queries.at[:, quarter[target]], q_send.at[k], q_recv.at[k], peer)

    swap, across, relay = move(0, 0, 1, twin), move(1, 0, 2, x_near), move(2, 2, 3, twin)

    def score(d, dy, quarters):
        passage = at((z + d) % 4, (y + dy) % 2, core) * 2 + x
        for k in range(quarters[0] * width // 256, (quarters[-1] + 1) * width // 256):
            cols = slice(k * 256, (k + 1) * 256)
            similar = jnp.dot(blocks[2 * d + dy], queries[:, cols], preferred_element_type=jnp.float32)
            best[pl.ds(passage, 1), cols] = jnp.max(similar, axis=0, keepdims=True)

    along_z[1].start()
    along_z[3].start()
    along_z[2].start()
    across.start()
    along_y[0].start()
    swap.start()
    score(0, 0, [0])
    for d in (1, 3):
        along_z[d].wait_recv()
        along_y[d].start()
    swap.wait_recv()
    score(0, 0, [1])
    score(1, 0, [0, 1])
    score(3, 0, [0, 1])
    along_z[2].wait_recv()
    along_y[2].start()
    along_y[0].wait_recv()
    score(0, 1, [0, 1])
    across.wait_recv()
    relay.start()
    score(2, 0, [0, 1])
    early = [(0, 0), (0, 1), (1, 0), (3, 0), (2, 0)]
    for d, dy in early:
        score(d, dy, [2])
    along_y[1].wait_recv()
    score(1, 1, [0, 2])
    relay.wait_recv()
    for d, dy in early + [(1, 1)]:
        score(d, dy, [3])
    for d in (3, 2):
        along_y[d].wait_recv()
        score(d, 1, [0, 3])

    group = jnp.where(member, 1.0, 0.0).astype(jnp.bfloat16)

    def total(values):
        high = values.astype(jnp.bfloat16)
        low = (values - high.astype(jnp.float32)).astype(jnp.bfloat16)
        dims = (((1,), (1,)), ((), ()))
        return lax.dot_general(group, high, dims, preferred_element_type=jnp.float32) + lax.dot_general(
            group, low, dims, preferred_element_type=jnp.float32
        )

    returns = []
    for k, peer in ((3, x_twin), (2, x_near), (1, twin)):
        part_out[k] = total(best[:, k * width : (k + 1) * width])
        back = remote(part_out.at[k], part_in.at[k], p_send.at[k], p_recv.at[k], peer)
        back.start()
        returns.append(back)
    mine = total(best[:, 0:width])
    for copy in list(along_z.values()) + list(along_y.values()) + [swap, across, relay]:
        copy.wait_send()
    for back in returns:
        back.wait()
    out_ref[...] = (mine + part_in[1]) + (part_in[2] + part_in[3])


def fused(query_hidden, query_mask, passage_hidden, passage_ids, passage_lengths, projection):
    qcount, qlen, depth = query_hidden.shape
    width = qcount * qlen
    rows = passage_hidden.shape[1]
    passages = PASS_GRP * lax.axis_size("gallery")
    anywhere = pl.BlockSpec(memory_space=pltpu.HBM)
    dma = pltpu.SemaphoreType.DMA
    bf16, f32 = jnp.bfloat16, jnp.float32
    return pl.pallas_call(
        fused_kernel,
        out_shape=jax.ShapeDtypeStruct((qcount, passages), f32),
        in_specs=[anywhere] * 6,
        out_specs=pl.BlockSpec(memory_space=pltpu.VMEM),
        scratch_shapes=[
            pltpu.VMEM((width, depth), bf16),
            pltpu.VMEM((qcount, qlen), jnp.int32),
            pltpu.VMEM((rows, depth), bf16),
            pltpu.VMEM((1, rows), jnp.int32),
            pltpu.SMEM(passage_lengths.shape, jnp.int32),
            pltpu.VMEM((depth, DIM), bf16),
            pltpu.VMEM((ROWS, DIM), f32),
            pltpu.VMEM((8, ROWS, DIM), bf16),
            pltpu.VMEM((DIM, 4 * width), bf16),
            pltpu.VMEM((passages, 4 * width), f32),
            pltpu.VMEM((4, qcount, passages), f32),
            pltpu.VMEM((4, qcount, passages), f32),
            dma((6,)), dma((4,)), dma((4,)), dma((4,)), dma((4,)), dma((3,)), dma((3,)), dma((4,)), dma((4,)),
        ],
        compiler_params=pltpu.CompilerParams(
            collective_id=0, has_side_effects=True, vmem_limit_bytes=60 * 1024 * 1024
        ),
    )(query_hidden.reshape(width, depth), query_mask, passage_hidden, passage_ids, passage_lengths, projection)


def solution(mesh):
    placed = (
        P(("query", "gallery"), None, None),
        P(("query", "gallery"), None),
        P("gallery", "query", None),
        P("gallery", "query"),
        P("gallery"),
        P(),
    )
    small = mesh.shape["query"] == PASS_GRP and mesh.shape["gallery"] == 16
    return jax.shard_map(
        fused if small else local, mesh=mesh, in_specs=placed, out_specs=P(("query", "gallery"), None), check_vma=False
    )
```
